256 devices in a mesh: region: 16 (over x, y), replica: 8 (over z), tensor: 2 (over core).
Axes of the slice: x: 4, y: 4, z: 8, core: 2. Of those that a mesh axis runs over, the one named last changes fastest.
Arguments:
- gradient: bfloat16 [8, 16, 8192, 256], P('replica', 'region', None, 'tensor'), parts along dimension 3, may hold values from -6 to 6
- feedback: float32 [8, 16, 8192, 256], P('replica', 'region', None, 'tensor'), parts along dimension 3, may hold values from -4 to 4
- picked: int32 [8, 16, 16, 128], P('replica', 'region', None, 'tensor'), parts along dimension 3, may hold values from 0 to 511, as said below
- counts: int32 [8, 16, 32], P('replica', 'region', 'tensor'), parts along dimension 2, may hold values from 0 to 64, as said below
- weights: float32 [8192, 256], P(('region', 'replica'), 'tensor'), parts along dimension 1, may hold values from -6 to 6
- moment: float32 [8192, 256], P(('region', 'replica'), 'tensor'), parts along dimension 1, may hold values from -3 to 3
- second: float32 [8192, 256], P(('region', 'replica'), 'tensor'), parts along dimension 1, may hold values from 0.01 to 1
Outputs:
- new_weights: float32 [8192, 256], P(('region', 'replica'), 'tensor'), parts along dimension 1
- new_moment: float32 [8192, 256], P(('region', 'replica'), 'tensor'), parts along dimension 1
- new_second: float32 [8192, 256], P(('region', 'replica'), 'tensor'), parts along dimension 1
- new_feedback: float32 [8, 16, 8192, 256], P('replica', 'region', None, 'tensor'), parts along dimension 3
The draws below stay inside these ranges and needn't reach their ends.
There are 2 independent parts, one for each index of `tensor`. The reference program is written for one: setup_inputs(seed, part) draws one part's arguments, and reference() takes and returns one part's arrays. A program takes and returns all parts, laid end to end along the dimension named above; each array names one. Nothing has to cross between parts.
Inputs may be any that keep to these rules, and one draw needn't show every extreme that they name: `picked`: for each worker and owner, 64 distinct block numbers within the owner's region; slots at or past the count are ignored. `counts`: in every replica some owner gets 64 live slots from every worker of the region.
All inputs are finite; a program needn't handle non-finite values.
Results may differ from the reference program's by a relative error of at most 0.0003.
Values sent between devices are 32-bit elements; how exact they have to be, the bound alone decides.
No kernel may reach another device: no remote copies, remote signals or barrier semaphores. Data moves between devices by JAX's collectives and lax.ppermute only.
A program may use at most 64 MiB of HBM per device.

```python
import math
import jax
import jax.numpy as jnp
from jax import lax

BLOCK = 128
REG_BLK = 512
CAP = 64
NBLK = 8192
N_REGION = 16
N_REPLICA = 8


def draw_picked(key, part):
    key = jax.random.fold_in(key, 23)
    scores = jax.random.randint(key, (N_REPLICA, N_REGION, N_REGION, REG_BLK), 0, 65536)
    scores = scores * REG_BLK + jnp.arange(REG_BLK, dtype=jnp.int32)
    order = jnp.argsort(scores, axis=-1)
    return order[..., :CAP].astype(jnp.int32)


def draw_counts(key, part):
    key = jax.random.fold_in(key, 11)
    key_level, key_count, key_hot = jax.random.split(key, 3)
    level = jax.random.randint(key_level, (N_REPLICA, 1, N_REGION), 1, CAP + 1)
    drawn = jax.random.randint(key_count, (N_REPLICA, N_REGION, N_REGION), 0, level + 1)
    hot_owner = jax.random.randint(key_hot, (N_REPLICA, 1, 1), 0, N_REGION)
    owners = jnp.arange(N_REGION, dtype=jnp.int32)[None, None, :]
    return jnp.where(owners == hot_owner, CAP, drawn).astype(jnp.int32)


def shard_levels(key, shape, shards, smallest, top_value):
    level, own = 1.0, jax.random.fold_in(key, 6)
    for position, blocks in shards:
        heights = jnp.exp(jax.random.uniform(jax.random.fold_in(own, position), (blocks,), jnp.float32, smallest / len(shards), top_value / len(shards)))
        level = level * jnp.repeat(heights, shape[position] // blocks).reshape([-1 if axis == position else 1 for axis in range(len(shape))])
    return level


def scatter_about(key, dims, width, limit, shards=(), kind=jnp.bfloat16):
    result = width * jax.random.normal(key, dims, jnp.float32)
    if shards:
        result = result * shard_levels(key, dims, shards, -0.22, 0.18)
    return jnp.clip(result, -limit, limit).astype(kind)


def setup_inputs(seed: int = 0, part: int = 0) -> dict:
    arg_keys = jax.random.split(jax.random.key(seed), 8)
    part_splits = jax.random.split(jax.random.fold_in(arg_keys[7], part), 8)
    gradient = scatter_about(part_splits[0], (N_REPLICA, N_REGION, NBLK, BLOCK), 1.0, 6.0, ((0, 8), (1, 16)))
    feedback = scatter_about(part_splits[1], (N_REPLICA, N_REGION, NBLK, BLOCK), 0.5, 4.0, ((0, 8), (1, 16)), jnp.float32)
    picked = draw_picked(jax.random.fold_in(jax.random.fold_in(arg_keys[7], part), 71), part)
    counts = draw_counts(jax.random.fold_in(jax.random.fold_in(arg_keys[7], part), 71), part)
    weights = scatter_about(part_splits[4], (NBLK, BLOCK), 1.0, 6.0, ((0, 128),), jnp.float32)
    moment = scatter_about(part_splits[5], (NBLK, BLOCK), 0.3, 3.0, ((0, 128),), jnp.float32)
    second = jnp.clip(jnp.exp(math.log(1.0) - 4.6051702 * jax.random.uniform(part_splits[6], (NBLK, BLOCK), jnp.float32) ** shard_levels(part_splits[6], (NBLK, BLOCK), ((0, 128),), -0.2, 0.2)), 0.01, 1.0)
    return {"gradient": gradient, "feedback": feedback, "picked": picked, "counts": counts, "weights": weights, "moment": moment, "second": second}


def reference(gradient, feedback, picked, counts, weights, moment, second):
    workers = N_REPLICA * N_REGION
    grad_rows = gradient.reshape(workers, NBLK, BLOCK)
    error_rows = feedback.reshape(workers, NBLK, BLOCK)
    slots = jnp.arange(CAP, dtype=jnp.int32)
    live = (slots[None, None, None, :] < counts[..., None]).reshape(workers, N_REGION * CAP)
    offsets = (jnp.arange(N_REGION, dtype=jnp.int32) * REG_BLK)[:, None]
    rows = (picked.reshape(workers, N_REGION, CAP) + offsets[None]).reshape(workers, N_REGION * CAP).astype(jnp.int32)

    def per_worker(items):
        grad_one, error_one, rows_one, live_one = items
        compensated = grad_one.astype(jnp.float32) + error_one
        keep = live_one.astype(jnp.float32)
        tiles = compensated[rows_one] * keep[:, None]
        flags = jnp.zeros((NBLK,), jnp.float32).at[rows_one].max(keep)
        return (tiles, compensated * (1.0 - flags)[:, None])
    tiles, fresh = lax.map(per_worker, (grad_rows, error_rows, rows, live))
    total = jnp.zeros((NBLK, BLOCK), jnp.float32).at[rows.reshape(-1)].add(tiles.reshape(-1, BLOCK))
    new_moment = 0.9 * moment + 0.1 * total
    new_second = 0.95 * second + 0.05 * total * total
    new_weights = weights - 0.02 * (new_moment / (jnp.sqrt(new_second) + 1e-08) + 0.1 * weights)
    new_feedback = fresh.reshape(N_REPLICA, N_REGION, NBLK, BLOCK)
    return (new_weights, new_moment, new_second, new_feedback)
```

```python
import functools

import jax
import jax.numpy as jnp
from jax import lax
from jax.experimental import pallas as pl
from jax.experimental.pallas import tpu as pltpu
from jax.sharding import PartitionSpec as P


def split(value):
    high = value.astype(jnp.bfloat16)
    low = (value - high.astype(jnp.float32)).astype(jnp.bfloat16)
    return jnp.concatenate([high, low], axis=1)


def one_hot(rows, ids):
    row = lax.broadcasted_iota(jnp.int32, (rows, ids.shape[1]), 0)
    return jnp.where(row == ids, 1.0, 0.0).astype(jnp.bfloat16)


def pack_kernel(counts, picked, gradient, feedback, tiles, new_feedback):
    owner = pl.program_id(0)
    slots = picked.shape[-1]
    rows, width = gradient.shape[2:]
    compensated = gradient[0, 0].astype(jnp.float32) + feedback[0, 0]
    slot = lax.broadcasted_iota(jnp.int32, (1, slots), 1)
    ids = jnp.where(slot < counts[0, 0, owner], picked[0, 0, pl.ds(owner, 1), :], -1)
    hot = one_hot(rows, ids)
    named = jnp.dot(hot, jnp.ones((slots, width), jnp.bfloat16), preferred_element_type=jnp.float32)
    new_feedback[0, 0] = jnp.where(named > 0.0, 0.0, compensated)
    halves = lax.dot_general(hot, split(compensated), (((0,), (0,)), ((), ())), preferred_element_type=jnp.float32)
    tiles[0, :slots, :] = halves[:, :width] + halves[:, width:]
    sent = ids.astype(jnp.float32)
    tiles[0, slots:, :] = jnp.broadcast_to(jnp.concatenate([sent, sent], axis=1), (tiles.shape[1] - slots, width))


def pack(counts, picked, gradient, feedback):
    owners, slots = picked.shape[2:]
    blocks, width = gradient.shape[2:]
    rows = blocks // owners
    whole = pl.BlockSpec((1, 1, rows, width), lambda o: (0, 0, o, 0))
    return pl.pallas_call(
        pack_kernel,
        grid=(owners,),
        in_specs=[
            pl.BlockSpec(memory_space=pltpu.SMEM),
            pl.BlockSpec((1, 1, owners, slots), lambda o: (0, 0, 0, 0)),
            whole,
            whole,
        ],
        out_specs=[pl.BlockSpec((1, slots + 8, width), lambda o: (o, 0, 0)), whole],
        out_shape=[
            jax.ShapeDtypeStruct((owners, slots + 8, width), jnp.float32),
            jax.ShapeDtypeStruct(feedback.shape, jnp.float32),
        ],
        compiler_params=pltpu.CompilerParams(vmem_limit_bytes=48 * 2**20),
        name="pack",
    )(counts, picked, gradient, feedback)


def gather_sum_kernel(slots, rows, got, kept, sent, hot, parts):
    me = lax.axis_index("replica")
    sources, _, width = got.shape
    lane = lax.broadcasted_iota(jnp.int32, (1, 2 * slots), 1)
    for pair in range(sources // 2):
        first, second = 2 * pair, 2 * pair + 1
        ids = jnp.where(lane < slots, got[first, slots : slots + 1, :], got[second, slots : slots + 1, :])
        ids = ids.astype(jnp.int32)
        far = (ids >> 6) ^ me
        place = jnp.where(ids < 0, -1, ((far & 1) << 8) | ((far >> 1) << 6) | (ids & 63))
        hot[:, pair * 2 * slots : (pair + 1) * 2 * slots] = one_hot(rows, place)
        for source in (first, second):
            parts[source * slots : (source + 1) * slots, :] = split(got[source, :slots, :])
    halves = jnp.dot(hot[...], parts[...], preferred_element_type=jnp.float32)
    total = halves[:, :width] + halves[:, width:]
    kept[...] = total[: rows // 2]
    sent[...] = total[rows // 2 :]


def gather_sum(got, rows):
    sources, _, width = got.shape
    slots = width // 2
    half = jax.ShapeDtypeStruct((rows // 2, width), jnp.float32)
    return pl.pallas_call(
        functools.partial(gather_sum_kernel, slots, rows),
        in_specs=[pl.BlockSpec(memory_space=pltpu.VMEM)],
        out_specs=[pl.BlockSpec(memory_space=pltpu.VMEM)] * 2,
        out_shape=[half, half],
        scratch_shapes=[
            pltpu.VMEM((rows, sources * slots), jnp.bfloat16),
            pltpu.VMEM((sources * slots, 2 * width), jnp.bfloat16),
        ],
        compiler_params=pltpu.CompilerParams(vmem_limit_bytes=48 * 2**20),
        name="gather_sum",
    )(got)


def swapped(value, mask):
    return lax.ppermute(value, "replica", [(source, source ^ mask) for source in range(lax.axis_size("replica"))])


def body(gradient, feedback, picked, counts, weights, moment, second):
    own_rows = weights.shape[0]
    reg_rows = own_rows * lax.axis_size("replica")
    tiles, new_feedback = pack(counts, picked, gradient, feedback)
    got = lax.all_to_all(tiles, "region", split_axis=0, concat_axis=0, tiled=True)
    kept, sent = gather_sum(got, reg_rows)
    part = (kept + swapped(sent, 1)).reshape(4, own_rows, kept.shape[1])
    far = [swapped(part[pair], 2 * pair) for pair in (2, 1, 3)]
    total = part[0] + far[0] + far[1] + far[2]
    new_moment = 0.9 * moment + 0.1 * total
    new_second = 0.95 * second + 0.05 * total * total
    new_weights = weights - 0.02 * (new_moment / (jnp.sqrt(new_second) + 1e-08) + 0.1 * weights)
    return (new_weights, new_moment, new_second, new_feedback)


def solution(mesh):
    placed = (
        P("replica", "region", None, "tensor"),
        P("replica", "region", None, "tensor"),
        P("replica", "region", None, "tensor"),
        P("replica", "region", "tensor"),
        P(("region", "replica"), "tensor"),
        P(("region", "replica"), "tensor"),
        P(("region", "replica"), "tensor"),
    )
    return jax.shard_map(
        body,
        mesh=mesh,
        in_specs=placed,
        out_specs=(
            P(("region", "replica"), "tensor"),
            P(("region", "replica"), "tensor"),
            P(("region", "replica"), "tensor"),
            P("replica", "region", None, "tensor"),
        ),
        check_vma=False,
    )
```

```python
import functools

import jax
import jax.numpy as jnp
from jax import lax
from jax.experimental import pallas as pl
from jax.experimental.pallas import tpu as pltpu
from jax.sharding import PartitionSpec as P


def split(value):
    high = value.astype(jnp.bfloat16)
    low = (value - high.astype(jnp.float32)).astype(jnp.bfloat16)
    return jnp.concatenate([high, low], axis=1)


def one_hot(rows, ids):
    row = lax.broadcasted_iota(jnp.int32, (rows, ids.shape[1]), 0)
    return jnp.where(row == ids, 1.0, 0.0).astype(jnp.bfloat16)


def pack_kernel(chunks, counts_in, picked_in, gradient, feedback, tiles, new_feedback, near, counts, picked, sems):
    owners, slots = picked.shape[2:]
    blocks, width = near.shape
    rows = blocks // owners
    step_rows = blocks // chunks

    def copies(chunk):
        here = pl.ds(pl.multiple_of(chunk * step_rows, step_rows), step_rows)
        return (
            pltpu.make_async_copy(gradient.at[0, 0, here, :], near.at[here, :], sems.at[0, chunk]),
            pltpu.make_async_copy(feedback.at[0, 0, here, :], new_feedback.at[0, 0, here, :], sems.at[1, chunk]),
        )

    lists = (
        pltpu.make_async_copy(counts_in, counts, sems.at[2, 0]),
        pltpu.make_async_copy(picked_in, picked, sems.at[2, 1]),
    )
    for copy in lists:
        copy.start()
    for chunk in range(chunks):
        for copy in copies(chunk):
            copy.start()
    for copy in lists:
        copy.wait()
    slot = lax.broadcasted_iota(jnp.int32, (1, slots), 1)

    def step(chunk, carry):
        for copy in copies(chunk):
            copy.wait()
        for part in range(owners // chunks):
            owner = chunk * (owners // chunks) + part
            here = pl.ds(pl.multiple_of(owner * rows, rows), rows)
            compensated = near[here, :].astype(jnp.float32) + new_feedback[0, 0, here, :]
            ids = jnp.where(slot < counts[0, 0, owner], picked[0, 0, pl.ds(owner, 1), :], -1)
            hot = one_hot(rows, ids)
            named = jnp.dot(hot, jnp.ones((slots, width), jnp.bfloat16), preferred_element_type=jnp.float32)
            new_feedback[0, 0, here, :] = jnp.where(named > 0.0, 0.0, compensated)
            halves = lax.dot_general(
                hot, split(compensated), (((0,), (0,)), ((), ())), preferred_element_type=jnp.float32
            )
            tiles[owner, :slots, :] = halves[:, :width] + halves[:, width:]
            sent = ids.astype(jnp.float32)
            sent = jnp.concatenate([sent, sent], axis=1)
            tiles[owner, slots:, :] = jnp.broadcast_to(sent, (tiles.shape[1] - slots, width))
        return carry

    lax.fori_loop(0, chunks, step, 0)


def pack(counts, picked, gradient, feedback):
    owners, slots = picked.shape[2:]
    blocks, width = gradient.shape[2:]
    chunks = 4
    arrays = [pltpu.with_memory_space_constraint(array, pltpu.HBM) for array in (counts, picked, gradient, feedback)]
    return pl.pallas_call(
        functools.partial(pack_kernel, chunks),
        in_specs=[pl.BlockSpec(memory_space=pltpu.HBM)] * 4,
        out_specs=[pl.BlockSpec(memory_space=pltpu.VMEM)] * 2,
        out_shape=[
            pltpu.VMEM((owners, slots + 8, width), jnp.float32),
            pltpu.VMEM(feedback.shape, jnp.float32),
        ],
        scratch_shapes=[
            pltpu.VMEM((blocks, width), jnp.bfloat16),
            pltpu.SMEM(counts.shape, jnp.int32),
            pltpu.VMEM(picked.shape, jnp.int32),
            pltpu.SemaphoreType.DMA((3, chunks)),
        ],
        compiler_params=pltpu.CompilerParams(vmem_limit_bytes=32 * 2**20),
        name="pack",
    )(*arrays)


def gather_sum_kernel(slots, rows, got, kept, sent, hot, parts):
    me = lax.axis_index("replica")
    sources, _, width = got.shape
    lane = lax.broadcasted_iota(jnp.int32, (1, 2 * slots), 1)
    for pair in range(sources // 2):
        first, second = 2 * pair, 2 * pair + 1
        ids = jnp.where(lane < slots, got[first, slots : slots + 1, :], got[second, slots : slots + 1, :])
        ids = ids.astype(jnp.int32)
        far = (ids >> 6) ^ me
        place = jnp.where(ids < 0, -1, ((far & 1) << 8) | ((far >> 1) << 6) | (ids & 63))
        hot[:, pair * 2 * slots : (pair + 1) * 2 * slots] = one_hot(rows, place)
        for source in (first, second):
            parts[source * slots : (source + 1) * slots, :] = split(got[source, :slots, :])
    halves = jnp.dot(hot[...], parts[...], preferred_element_type=jnp.float32)
    total = halves[:, :width] + halves[:, width:]
    kept[...] = total[: rows // 2]
    sent[...] = total[rows // 2 :]


def gather_sum(got, rows):
    sources, _, width = got.shape
    slots = width // 2
    half = jax.ShapeDtypeStruct((rows // 2, width), jnp.float32)
    return pl.pallas_call(
        functools.partial(gather_sum_kernel, slots, rows),
        in_specs=[pl.BlockSpec(memory_space=pltpu.VMEM)],
        out_specs=[pl.BlockSpec(memory_space=pltpu.VMEM)] * 2,
        out_shape=[half, half],
        scratch_shapes=[
            pltpu.VMEM((rows, sources * slots), jnp.bfloat16),
            pltpu.VMEM((sources * slots, 2 * width), jnp.bfloat16),
        ],
        compiler_params=pltpu.CompilerParams(vmem_limit_bytes=48 * 2**20),
        name="gather_sum",
    )(got)


def swapped(value, mask):
    return lax.ppermute(value, "replica", [(source, source ^ mask) for source in range(lax.axis_size("replica"))])


def body(gradient, feedback, picked, counts, weights, moment, second):
    own_rows = weights.shape[0]
    reg_rows = own_rows * lax.axis_size("replica")
    tiles, new_feedback = pack(counts, picked, gradient, feedback)
    got = lax.all_to_all(tiles, "region", split_axis=0, concat_axis=0, tiled=True)
    kept, sent = gather_sum(got, reg_rows)
    part = (kept + swapped(sent, 1)).reshape(4, own_rows, kept.shape[1])
    far = [swapped(part[pair], 2 * pair) for pair in (2, 1, 3)]
    total = part[0] + far[0] + far[1] + far[2]
    new_moment = 0.9 * moment + 0.1 * total
    new_second = 0.95 * second + 0.05 * total * total
    new_weights = weights - 0.02 * (new_moment / (jnp.sqrt(new_second) + 1e-08) + 0.1 * weights)
    return (new_weights, new_moment, new_second, new_feedback)


def solution(mesh):
    placed = (
        P("replica", "region", None, "tensor"),
        P("replica", "region", None, "tensor"),
        P("replica", "region", None, "tensor"),
        P("replica", "region", "tensor"),
        P(("region", "replica"), "tensor"),
        P(("region", "replica"), "tensor"),
        P(("region", "replica"), "tensor"),
    )
    return jax.shard_map(
        body,
        mesh=mesh,
        in_specs=placed,
        out_specs=(
            P(("region", "replica"), "tensor"),
            P(("region", "replica"), "tensor"),
            P(("region", "replica"), "tensor"),
            P("replica", "region", None, "tensor"),
        ),
        check_vma=False,
    )
```

```python
import functools

import jax
import jax.numpy as jnp
from jax import lax
from jax.experimental import pallas as pl
from jax.experimental.pallas import tpu as pltpu
from jax.sharding import PartitionSpec as P


def split(value):
    high = value.astype(jnp.bfloat16)
    low = (value - high.astype(jnp.float32)).astype(jnp.bfloat16)
    return jnp.concatenate([high, low], axis=1)


def one_hot(rows, ids):
    row = lax.broadcasted_iota(jnp.int32, (rows, ids.shape[1]), 0)
    return jnp.where(row == ids, 1.0, 0.0).astype(jnp.bfloat16)


def pack_kernel(chunks, counts_in, picked_in, gradient, feedback, tiles, new_feedback, near, counts, picked, sems):
    owners, slots = picked.shape[2:]
    blocks, width = near.shape
    rows = blocks // owners
    step_rows = blocks // chunks

    def copies(chunk):
        here = pl.ds(pl.multiple_of(chunk * step_rows, step_rows), step_rows)
        return (
            pltpu.make_async_copy(gradient.at[0, 0, here, :], near.at[here, :], sems.at[0, chunk]),
            pltpu.make_async_copy(feedback.at[0, 0, here, :], new_feedback.at[0, 0, here, :], sems.at[1, chunk]),
        )

    lists = (
        pltpu.make_async_copy(counts_in, counts, sems.at[2, 0]),
        pltpu.make_async_copy(picked_in, picked, sems.at[2, 1]),
    )
    for copy in lists:
        copy.start()
    for chunk in range(chunks):
        for copy in copies(chunk):
            copy.start()
    for copy in lists:
        copy.wait()
    slot = lax.broadcasted_iota(jnp.int32, (1, slots), 1)

    def step(chunk, carry):
        for copy in copies(chunk):
            copy.wait()
        for part in range(owners // chunks):
            owner = chunk * (owners // chunks) + part
            here = pl.ds(pl.multiple_of(owner * rows, rows), rows)
            compensated = near[here, :].astype(jnp.float32) + new_feedback[0, 0, here, :]
            ids = jnp.where(slot < counts[0, 0, owner], picked[0, 0, pl.ds(owner, 1), :], -1)
            hot = one_hot(rows, ids)
            named = jnp.dot(hot, jnp.ones((slots, width), jnp.bfloat16), preferred_element_type=jnp.float32)
            new_feedback[0, 0, here, :] = jnp.where(named > 0.0, 0.0, compensated)
            halves = lax.dot_general(
                hot, split(compensated), (((0,), (0,)), ((), ())), preferred_element_type=jnp.float32
            )
            tiles[owner, :slots, :] = halves[:, :width] + halves[:, width:]
            sent = ids.astype(jnp.float32)
            sent = jnp.concatenate([sent, sent], axis=1)
            tiles[owner, slots:, :] = jnp.broadcast_to(sent, (tiles.shape[1] - slots, width))
        return carry

    lax.fori_loop(0, chunks, step, 0)


def pack(counts, picked, gradient, feedback):
    owners, slots = picked.shape[2:]
    blocks, width = gradient.shape[2:]
    chunks = 4
    arrays = [pltpu.with_memory_space_constraint(array, pltpu.HBM) for array in (counts, picked, gradient, feedback)]
    return pl.pallas_call(
        functools.partial(pack_kernel, chunks),
        in_specs=[pl.BlockSpec(memory_space=pltpu.HBM)] * 4,
        out_specs=[pl.BlockSpec(memory_space=pltpu.VMEM)] * 2,
        out_shape=[
            pltpu.VMEM((owners, slots + 8, width), jnp.float32),
            pltpu.VMEM(feedback.shape, jnp.float32),
        ],
        scratch_shapes=[
            pltpu.VMEM((blocks, width), jnp.bfloat16),
            pltpu.SMEM(counts.shape, jnp.int32),
            pltpu.VMEM(picked.shape, jnp.int32),
            pltpu.SemaphoreType.DMA((3, chunks)),
        ],
        compiler_params=pltpu.CompilerParams(vmem_limit_bytes=32 * 2**20),
        name="pack",
    )(*arrays)


def gather_sum_kernel(slots, rows, got, kept_first, kept, sent_first, sent, hot, parts):
    me = lax.axis_index("replica")
    sources, _, width = got.shape
    block = kept_first.shape[0]
    lane = lax.broadcasted_iota(jnp.int32, (1, 2 * slots), 1)
    for pair in range(sources // 2):
        first, second = 2 * pair, 2 * pair + 1
        ids = jnp.where(lane < slots, got[first, slots : slots + 1, :], got[second, slots : slots + 1, :])
        ids = ids.astype(jnp.int32)
        far = (ids >> 6) ^ me
        two, one = far >> 2, (far >> 1) & 1
        away = (far & 1) ^ two ^ (two & one)
        place = jnp.where(ids < 0, -1, (away << 8) | (one << 7) | ((1 - two) << 6) | (ids & 63))
        hot[:, pair * 2 * slots : (pair + 1) * 2 * slots] = one_hot(rows, place)
        for source in (first, second):
            parts[source * slots : (source + 1) * slots, :] = split(got[source, :slots, :])
    halves = jnp.dot(hot[...], parts[...], preferred_element_type=jnp.float32)
    total = halves[:, :width] + halves[:, width:]
    kept_first[...] = total[:block]
    kept[...] = total[block : rows // 2]
    sent_first[...] = total[rows // 2 : rows // 2 + block]
    sent[...] = total[rows // 2 + block :]


def gather_sum(got, rows):
    sources, _, width = got.shape
    slots = width // 2
    shapes = [jax.ShapeDtypeStruct((rows // 4, width), jnp.float32)] * 4
    return pl.pallas_call(
        functools.partial(gather_sum_kernel, slots, rows),
        in_specs=[pl.BlockSpec(memory_space=pltpu.VMEM)],
        out_specs=[pl.BlockSpec(memory_space=pltpu.VMEM)] * 4,
        out_shape=shapes,
        scratch_shapes=[
            pltpu.VMEM((rows, sources * slots), jnp.bfloat16),
            pltpu.VMEM((sources * slots, 2 * width), jnp.bfloat16),
        ],
        compiler_params=pltpu.CompilerParams(vmem_limit_bytes=16 * 2**20),
        name="gather_sum",
    )(got)


def swapped(value, mask):
    return lax.ppermute(value, "replica", [(source, source ^ mask) for source in range(lax.axis_size("replica"))])


def body(gradient, feedback, picked, counts, weights, moment, second):
    own_rows = weights.shape[0]
    reg_rows = own_rows * lax.axis_size("replica")
    tiles, new_feedback = pack(counts, picked, gradient, feedback)
    got = lax.all_to_all(tiles, "region", split_axis=0, concat_axis=0, tiled=True)
    kept_first, kept, sent_first, sent = gather_sum(got, reg_rows)
    five, own = jnp.split(kept_first + swapped(sent_first, 1), 2)
    six, two = jnp.split(kept + swapped(sent, 1), 2)
    total = own + swapped(five, 5) + swapped(six, 6) + swapped(two, 2)
    new_moment = 0.9 * moment + 0.1 * total
    new_second = 0.95 * second + 0.05 * total * total
    new_weights = weights - 0.02 * (new_moment / (jnp.sqrt(new_second) + 1e-08) + 0.1 * weights)
    return (new_weights, new_moment, new_second, new_feedback)


def solution(mesh):
    placed = (
        P("replica", "region", None, "tensor"),
        P("replica", "region", None, "tensor"),
        P("replica", "region", None, "tensor"),
        P("replica", "region", "tensor"),
        P(("region", "replica"), "tensor"),
        P(("region", "replica"), "tensor"),
        P(("region", "replica"), "tensor"),
    )
    return jax.shard_map(
        body,
        mesh=mesh,
        in_specs=placed,
        out_specs=(
            P(("region", "replica"), "tensor"),
            P(("region", "replica"), "tensor"),
            P(("region", "replica"), "tensor"),
            P("replica", "region", None, "tensor"),
        ),
        check_vma=False,
    )
```

```python
import functools

import jax
import jax.numpy as jnp
from jax import lax
from jax.experimental import pallas as pl
from jax.experimental.pallas import tpu as pltpu
from jax.sharding import PartitionSpec as P


def split(value):
    high = value.astype(jnp.bfloat16)
    low = (value - high.astype(jnp.float32)).astype(jnp.bfloat16)
    return jnp.concatenate([high, low], axis=1)


def one_hot(rows, ids):
    row = lax.broadcasted_iota(jnp.int32, (rows, ids.shape[1]), 0)
    return jnp.where(row == ids, 1.0, 0.0).astype(jnp.bfloat16)


def pack_kernel(chunks, counts_in, picked_in, gradient, feedback, tiles, new_feedback, near, counts, picked, sems):
    owners, slots = picked.shape[2:]
    blocks, width = near.shape
    rows = blocks // owners
    step_rows = blocks // chunks

    def copies(chunk):
        here = pl.ds(pl.multiple_of(chunk * step_rows, step_rows), step_rows)
        return (
            pltpu.make_async_copy(gradient.at[0, 0, here, :], near.at[here, :], sems.at[0, chunk]),
            pltpu.make_async_copy(feedback.at[0, 0, here, :], new_feedback.at[0, 0, here, :], sems.at[1, chunk]),
        )

    lists = (
        pltpu.make_async_copy(counts_in, counts, sems.at[2, 0]),
        pltpu.make_async_copy(picked_in, picked, sems.at[2, 1]),
    )
    for copy in lists:
        copy.start()
    for chunk in range(chunks):
        for copy in copies(chunk):
            copy.start()
    for copy in lists:
        copy.wait()
    slot = lax.broadcasted_iota(jnp.int32, (1, slots), 1)

    def step(chunk, carry):
        for copy in copies(chunk):
            copy.wait()
        for part in range(owners // chunks):
            owner = chunk * (owners // chunks) + part
            here = pl.ds(pl.multiple_of(owner * rows, rows), rows)
            compensated = near[here, :].astype(jnp.float32) + new_feedback[0, 0, here, :]
            ids = jnp.where(slot < counts[0, 0, owner], picked[0, 0, pl.ds(owner, 1), :], -1)
            hot = one_hot(rows, ids)
            named = jnp.dot(hot, jnp.ones((slots, width), jnp.bfloat16), preferred_element_type=jnp.float32)
            new_feedback[0, 0, here, :] = jnp.where(named > 0.0, 0.0, compensated)
            halves = lax.dot_general(
                hot, split(compensated), (((0,), (0,)), ((), ())), preferred_element_type=jnp.float32
            )
            tiles[owner, :slots, :] = halves[:, :width] + halves[:, width:]
            sent = ids.astype(jnp.float32)
            sent = jnp.concatenate([sent, sent], axis=1)
            tiles[owner, slots:, :] = jnp.broadcast_to(sent, (tiles.shape[1] - slots, width))
        return carry

    lax.fori_loop(0, chunks, step, 0)


def pack(counts, picked, gradient, feedback):
    owners, slots = picked.shape[2:]
    blocks, width = gradient.shape[2:]
    chunks = 4
    arrays = [pltpu.with_memory_space_constraint(array, pltpu.HBM) for array in (counts, picked, gradient, feedback)]
    return pl.pallas_call(
        functools.partial(pack_kernel, chunks),
        in_specs=[pl.BlockSpec(memory_space=pltpu.HBM)] * 4,
        out_specs=[pl.BlockSpec(memory_space=pltpu.VMEM)] * 2,
        out_shape=[
            pltpu.VMEM((owners, slots + 8, width), jnp.float32),
            pltpu.VMEM(feedback.shape, jnp.float32),
        ],
        scratch_shapes=[
            pltpu.VMEM((blocks, width), jnp.bfloat16),
            pltpu.SMEM(counts.shape, jnp.int32),
            pltpu.VMEM(picked.shape, jnp.int32),
            pltpu.SemaphoreType.DMA((3, chunks)),
        ],
        compiler_params=pltpu.CompilerParams(vmem_limit_bytes=32 * 2**20),
        name="pack",
    )(*arrays)


def gather_sum_kernel(slots, blocks, got, hot, parts, *sums):
    me = lax.axis_index("replica")
    sources, _, width = got.shape
    rows = hot.shape[0]
    own_rows = rows // 8
    lane = lax.broadcasted_iota(jnp.int32, (1, 2 * slots), 1)
    for pair in range(sources // 2):
        first, second = 2 * pair, 2 * pair + 1
        ids = jnp.where(lane < slots, got[first, slots : slots + 1, :], got[second, slots : slots + 1, :])
        ids = ids.astype(jnp.int32)
        place = jnp.where(ids < 0, -1, ids ^ (me * own_rows))
        hot[:, pair * 2 * slots : (pair + 1) * 2 * slots] = one_hot(rows, place)
        for source in (first, second):
            parts[source * slots : (source + 1) * slots, :] = split(got[source, :slots, :])
    halves = jnp.dot(hot[...], parts[...], preferred_element_type=jnp.float32)
    total = halves[:, :width] + halves[:, width:]
    for group, ref in zip(blocks, sums):
        for position, block in enumerate(group):
            here = slice(position * own_rows, (position + 1) * own_rows)
            ref[here, :] = total[block * own_rows : (block + 1) * own_rows]


def gather_sum(got, rows, blocks):
    sources, _, width = got.shape
    slots = width // 2

    def kernel(got, *refs):
        gather_sum_kernel(slots, blocks, got, *refs[-2:], *refs[:-2])

    return pl.pallas_call(
        kernel,
        in_specs=[pl.BlockSpec(memory_space=pltpu.VMEM)],
        out_specs=[pl.BlockSpec(memory_space=pltpu.VMEM)] * len(blocks),
        out_shape=[pltpu.VMEM((len(group) * rows // 8, width), jnp.float32) for group in blocks],
        scratch_shapes=[
            pltpu.VMEM((rows, sources * slots), jnp.bfloat16),
            pltpu.VMEM((sources * slots, 2 * width), jnp.bfloat16),
        ],
        compiler_params=pltpu.CompilerParams(vmem_limit_bytes=16 * 2**20),
        name="gather_sum",
    )(got)


def swapped(value, mask):
    return lax.ppermute(value, "replica", [(source, source ^ mask) for source in range(lax.axis_size("replica"))])


def body(gradient, feedback, picked, counts, weights, moment, second):
    own_rows = weights.shape[0]
    reg_rows = own_rows * lax.axis_size("replica")
    tiles, new_feedback = pack(counts, picked, gradient, feedback)
    got = lax.all_to_all(tiles, "region", split_axis=0, concat_axis=0, tiled=True)
    five, near, four, six, two, three, own = gather_sum(got, reg_rows, ((5,), (7, 1), (4,), (6,), (2,), (3,), (0,)))
    five = swapped(five, 3)
    near = swapped(near, 1)
    six = six + five + near[:own_rows] + swapped(four, 2)
    total = own + near[own_rows:] + swapped(six, 6) + swapped(two, 2) + swapped(three, 3)
    new_moment = 0.9 * moment + 0.1 * total
    new_second = 0.95 * second + 0.05 * total * total
    new_weights = weights - 0.02 * (new_moment / (jnp.sqrt(new_second) + 1e-08) + 0.1 * weights)
    return (new_weights, new_moment, new_second, new_feedback)


def solution(mesh):
    placed = (
        P("replica", "region", None, "tensor"),
        P("replica", "region", None, "tensor"),
        P("replica", "region", None, "tensor"),
        P("replica", "region", "tensor"),
        P(("region", "replica"), "tensor"),
        P(("region", "replica"), "tensor"),
        P(("region", "replica"), "tensor"),
    )
    return jax.shard_map(
        body,
        mesh=mesh,
        in_specs=placed,
        out_specs=(
            P(("region", "replica"), "tensor"),
            P(("region", "replica"), "tensor"),
            P(("region", "replica"), "tensor"),
            P("replica", "region", None, "tensor"),
        ),
        check_vma=False,
    )
```

```python
import functools

import jax
import jax.numpy as jnp
from jax import lax
from jax.experimental import pallas as pl
from jax.experimental.pallas import tpu as pltpu
from jax.sharding import PartitionSpec as P


def split(value):
    high = value.astype(jnp.bfloat16)
    low = (value - high.astype(jnp.float32)).astype(jnp.bfloat16)
    return jnp.concatenate([high, low], axis=1)


def one_hot(rows, ids):
    row = lax.broadcasted_iota(jnp.int32, (rows, ids.shape[1]), 0)
    return jnp.where(row == ids, 1.0, 0.0).astype(jnp.bfloat16)


def pack_kernel(chunks, counts_in, picked_in, gradient, feedback, tiles, new_feedback, near, counts, picked, hot, sems):
    owners, slots = picked.shape[2:]
    blocks, width = near.shape
    rows = blocks // owners
    step_rows = blocks // chunks
    pairs = owners // chunks // 2

    def copies(chunk):
        here = pl.ds(pl.multiple_of(chunk * step_rows, step_rows), step_rows)
        return (
            pltpu.make_async_copy(gradient.at[0, 0, here, :], near.at[here, :], sems.at[0, chunk]),
            pltpu.make_async_copy(feedback.at[0, 0, here, :], new_feedback.at[0, 0, here, :], sems.at[1, chunk]),
        )

    lists = (
        pltpu.make_async_copy(counts_in, counts, sems.at[2, 0]),
        pltpu.make_async_copy(picked_in, picked, sems.at[2, 1]),
    )
    for copy in lists:
        copy.start()
    for chunk in range(chunks):
        for copy in copies(chunk):
            copy.start()
    for copy in lists:
        copy.wait()
    lane = lax.broadcasted_iota(jnp.int32, (1, 2 * slots), 1)
    wide = (tiles.shape[1] - slots, 2 * slots)
    lower = lax.broadcasted_iota(jnp.int32, wide, 1) < slots

    def prepare(pair, carry):
        first, second = 2 * pair, 2 * pair + 1
        ids = jnp.concatenate([picked[0, 0, pl.ds(first, 1), :], picked[0, 0, pl.ds(second, 1), :]], axis=1)
        limit = jnp.where(lane < slots, counts[0, 0, first], counts[0, 0, second] + slots)
        ids = jnp.where(lane < limit, ids, -1)
        hot[pair] = one_hot(rows, ids)
        sent = jnp.broadcast_to(ids.astype(jnp.float32), wide)
        turned = pltpu.roll(sent, slots, 1)
        tiles[first, slots:, :] = jnp.where(lower, sent, turned)
        tiles[second, slots:, :] = jnp.where(lower, turned, sent)
        return carry

    lax.fori_loop(0, owners // 2, prepare, 0, unroll=4)
    lower = lax.broadcasted_iota(jnp.int32, (2 * slots, width), 0) < slots
    ones = (jnp.where(lower, 1.0, 0.0).astype(jnp.bfloat16), jnp.where(lower, 0.0, 1.0).astype(jnp.bfloat16))

    def step(chunk, carry):
        for copy in copies(chunk):
            copy.wait()
        for part in range(2 * pairs):
            pair, side = chunk * pairs + part // 2, part % 2
            owner = 2 * pair + side
            here = pl.ds(pl.multiple_of(owner * rows, rows), rows)
            compensated = near[here, :].astype(jnp.float32) + new_feedback[0, 0, here, :]
            both = hot[pair]
            named = jnp.dot(both, ones[side], preferred_element_type=jnp.float32)
            new_feedback[0, 0, here, :] = jnp.where(named > 0.0, 0.0, compensated)
            halves = lax.dot_general(
                both, split(compensated), (((0,), (0,)), ((), ())), preferred_element_type=jnp.float32
            )[side * slots : (side + 1) * slots]
            tiles[owner, :slots, :] = halves[:, :width] + halves[:, width:]
        return carry

    lax.fori_loop(0, chunks, step, 0)


def pack(counts, picked, gradient, feedback):
    owners, slots = picked.shape[2:]
    blocks, width = gradient.shape[2:]
    chunks = 4
    arrays = [pltpu.with_memory_space_constraint(array, pltpu.HBM) for array in (counts, picked, gradient, feedback)]
    return pl.pallas_call(
        functools.partial(pack_kernel, chunks),
        in_specs=[pl.BlockSpec(memory_space=pltpu.HBM)] * 4,
        out_specs=[pl.BlockSpec(memory_space=pltpu.VMEM)] * 2,
        out_shape=[
            pltpu.VMEM((owners, slots + 8, width), jnp.float32),
            pltpu.VMEM(feedback.shape, jnp.float32),
        ],
        scratch_shapes=[
            pltpu.VMEM((blocks, width), jnp.bfloat16),
            pltpu.SMEM(counts.shape, jnp.int32),
            pltpu.VMEM(picked.shape, jnp.int32),
            pltpu.VMEM((owners // 2, blocks // owners, 2 * slots), jnp.bfloat16),
            pltpu.SemaphoreType.DMA((3, chunks)),
        ],
        compiler_params=pltpu.CompilerParams(vmem_limit_bytes=32 * 2**20),
        name="pack",
    )(*arrays)


def gather_sum_kernel(slots, blocks, got, hot, parts, *sums):
    me = lax.axis_index("replica")
    sources, _, width = got.shape
    rows = hot.shape[0]
    own_rows = rows // 8
    lane = lax.broadcasted_iota(jnp.int32, (1, 2 * slots), 1)
    for pair in range(sources // 2):
        first, second = 2 * pair, 2 * pair + 1
        ids = jnp.where(lane < slots, got[first, slots : slots + 1, :], got[second, slots : slots + 1, :])
        ids = ids.astype(jnp.int32)
        place = jnp.where(ids < 0, -1, ids ^ (me * own_rows))
        hot[:, pair * 2 * slots : (pair + 1) * 2 * slots] = one_hot(rows, place)
        for source in (first, second):
            parts[source * slots : (source + 1) * slots, :] = split(got[source, :slots, :])
    halves = jnp.dot(hot[...], parts[...], preferred_element_type=jnp.float32)
    total = halves[:, :width] + halves[:, width:]
    for group, ref in zip(blocks, sums):
        for position, block in enumerate(group):
            here = slice(position * own_rows, (position + 1) * own_rows)
            ref[here, :] = total[block * own_rows : (block + 1) * own_rows]


def gather_sum(got, rows, blocks):
    sources, _, width = got.shape
    slots = width // 2

    def kernel(got, *refs):
        gather_sum_kernel(slots, blocks, got, *refs[-2:], *refs[:-2])

    return pl.pallas_call(
        kernel,
        in_specs=[pl.BlockSpec(memory_space=pltpu.VMEM)],
        out_specs=[pl.BlockSpec(memory_space=pltpu.VMEM)] * len(blocks),
        out_shape=[pltpu.VMEM((len(group) * rows // 8, width), jnp.float32) for group in blocks],
        scratch_shapes=[
            pltpu.VMEM((rows, sources * slots), jnp.bfloat16),
            pltpu.VMEM((sources * slots, 2 * width), jnp.bfloat16),
        ],
        compiler_params=pltpu.CompilerParams(vmem_limit_bytes=16 * 2**20),
        name="gather_sum",
    )(got)


def swapped(value, mask):
    return lax.ppermute(value, "replica", [(source, source ^ mask) for source in range(lax.axis_size("replica"))])


def body(gradient, feedback, picked, counts, weights, moment, second):
    own_rows = weights.shape[0]
    reg_rows = own_rows * lax.axis_size("replica")
    tiles, new_feedback = pack(counts, picked, gradient, feedback)
    got = lax.all_to_all(tiles, "region", split_axis=0, concat_axis=0, tiled=True)
    five, near, four, six, two, three, own = gather_sum(got, reg_rows, ((5,), (7, 1), (4,), (6,), (2,), (3,), (0,)))
    five = swapped(five, 3)
    near = swapped(near, 1)
    six = six + five + near[:own_rows] + swapped(four, 2)
    total = own + near[own_rows:] + swapped(six, 6) + swapped(two, 2) + swapped(three, 3)
    new_moment = 0.9 * moment + 0.1 * total
    new_second = 0.95 * second + 0.05 * total * total
    new_weights = weights - 0.02 * (new_moment / (jnp.sqrt(new_second) + 1e-08) + 0.1 * weights)
    return (new_weights, new_moment, new_second, new_feedback)


def solution(mesh):
    placed = (
        P("replica", "region", None, "tensor"),
        P("replica", "region", None, "tensor"),
        P("replica", "region", None, "tensor"),
        P("replica", "region", "tensor"),
        P(("region", "replica"), "tensor"),
        P(("region", "replica"), "tensor"),
        P(("region", "replica"), "tensor"),
    )
    return jax.shard_map(
        body,
        mesh=mesh,
        in_specs=placed,
        out_specs=(
            P(("region", "replica"), "tensor"),
            P(("region", "replica"), "tensor"),
            P(("region", "replica"), "tensor"),
            P("replica", "region", None, "tensor"),
        ),
        check_vma=False,
    )
```

```python
import functools

import jax
import jax.numpy as jnp
from jax import lax
from jax.experimental import pallas as pl
from jax.experimental.pallas import tpu as pltpu
from jax.sharding import PartitionSpec as P


def split(value):
    high = value.astype(jnp.bfloat16)
    low = (value - high.astype(jnp.float32)).astype(jnp.bfloat16)
    return jnp.concatenate([high, low], axis=1)


def one_hot(rows, ids):
    row = lax.broadcasted_iota(jnp.int32, (rows, ids.shape[1]), 0)
    return jnp.where(row == ids, 1.0, 0.0).astype(jnp.bfloat16)


def pack_kernel(chunks, counts_in, picked_in, gradient, feedback, tiles, new_feedback, near, counts, picked, hot, sems):
    owners, slots = picked.shape[2:]
    blocks, width = near.shape
    rows = blocks // owners
    step_rows = blocks // chunks
    pairs = owners // chunks // 2

    def copies(chunk):
        here = pl.ds(pl.multiple_of(chunk * step_rows, step_rows), step_rows)
        return (
            pltpu.make_async_copy(gradient.at[0, 0, here, :], near.at[here, :], sems.at[0, chunk]),
            pltpu.make_async_copy(feedback.at[0, 0, here, :], new_feedback.at[0, 0, here, :], sems.at[1, chunk]),
        )

    lists = (
        pltpu.make_async_copy(counts_in, counts, sems.at[2, 0]),
        pltpu.make_async_copy(picked_in, picked, sems.at[2, 1]),
    )
    for copy in lists:
        copy.start()
    for chunk in range(chunks):
        for copy in copies(chunk):
            copy.start()
    for copy in lists:
        copy.wait()
    lane = lax.broadcasted_iota(jnp.int32, (1, 2 * slots), 1)
    wide = (tiles.shape[1] - slots, 2 * slots)
    lower = lax.broadcasted_iota(jnp.int32, wide, 1) < slots

    def prepare(pair, carry):
        first, second = 2 * pair, 2 * pair + 1
        ids = jnp.concatenate([picked[0, 0, pl.ds(first, 1), :], picked[0, 0, pl.ds(second, 1), :]], axis=1)
        limit = jnp.where(lane < slots, counts[0, 0, first], counts[0, 0, second] + slots)
        ids = jnp.where(lane < limit, ids, -1)
        hot[pair] = one_hot(rows, ids)
        sent = jnp.broadcast_to(ids.astype(jnp.float32), wide)
        turned = pltpu.roll(sent, slots, 1)
        tiles[first, slots:, :] = jnp.where(lower, sent, turned)
        tiles[second, slots:, :] = jnp.where(lower, turned, sent)
        return carry

    lax.fori_loop(0, owners // 2, prepare, 0, unroll=4)
    lower = lax.broadcasted_iota(jnp.int32, (2 * slots, width), 0) < slots
    ones = (jnp.where(lower, 1.0, 0.0).astype(jnp.bfloat16), jnp.where(lower, 0.0, 1.0).astype(jnp.bfloat16))

    def step(chunk, carry):
        for copy in copies(chunk):
            copy.wait()
        for part in range(2 * pairs):
            pair, side = chunk * pairs + part // 2, part % 2
            owner = 2 * pair + side
            here = pl.ds(pl.multiple_of(owner * rows, rows), rows)
            compensated = near[here, :].astype(jnp.float32) + new_feedback[0, 0, here, :]
            both = hot[pair]
            named = jnp.dot(both, ones[side], preferred_element_type=jnp.float32)
            new_feedback[0, 0, here, :] = jnp.where(named > 0.0, 0.0, compensated)
            halves = lax.dot_general(
                both, split(compensated), (((0,), (0,)), ((), ())), preferred_element_type=jnp.float32
            )[side * slots : (side + 1) * slots]
            tiles[owner, :slots, :] = halves[:, :width] + halves[:, width:]
        return carry

    lax.fori_loop(0, chunks, step, 0)


def pack(counts, picked, gradient, feedback):
    owners, slots = picked.shape[2:]
    blocks, width = gradient.shape[2:]
    chunks = 4
    arrays = [pltpu.with_memory_space_constraint(array, pltpu.HBM) for array in (counts, picked, gradient, feedback)]
    return pl.pallas_call(
        functools.partial(pack_kernel, chunks),
        in_specs=[pl.BlockSpec(memory_space=pltpu.HBM)] * 4,
        out_specs=[pl.BlockSpec(memory_space=pltpu.VMEM)] * 2,
        out_shape=[
            pltpu.VMEM((owners, slots + 8, width), jnp.float32),
            pltpu.VMEM(feedback.shape, jnp.float32),
        ],
        scratch_shapes=[
            pltpu.VMEM((blocks, width), jnp.bfloat16),
            pltpu.SMEM(counts.shape, jnp.int32),
            pltpu.VMEM(picked.shape, jnp.int32),
            pltpu.VMEM((owners // 2, blocks // owners, 2 * slots), jnp.bfloat16),
            pltpu.SemaphoreType.DMA((3, chunks)),
        ],
        compiler_params=pltpu.CompilerParams(vmem_limit_bytes=32 * 2**20),
        name="pack",
    )(*arrays)


def gather_sum_kernel(slots, rows, blocks, got, *sums):
    me = lax.axis_index("replica")
    sources, _, width = got.shape
    own_rows = rows // 8
    lane = lax.broadcasted_iota(jnp.int32, (1, 2 * slots), 1)

    def hot(pair):
        first, second = 2 * pair, 2 * pair + 1
        ids = jnp.where(lane < slots, got[first, slots : slots + 1, :], got[second, slots : slots + 1, :])
        ids = ids.astype(jnp.int32)
        return one_hot(rows, jnp.where(ids < 0, -1, ids ^ (me * own_rows)))

    halves = jnp.zeros((rows, 2 * width), jnp.float32)
    for pair in range(0, sources // 2, 2):
        named = jnp.concatenate([hot(pair), hot(pair + 1)], axis=1)
        parts = [split(got[source, :slots, :]) for source in range(2 * pair, 2 * pair + 4)]
        halves += jnp.dot(named, jnp.concatenate(parts, axis=0), preferred_element_type=jnp.float32)
    total = halves[:, :width] + halves[:, width:]
    for group, ref in zip(blocks, sums):
        for position, block in enumerate(group):
            here = slice(position * own_rows, (position + 1) * own_rows)
            ref[here, :] = total[block * own_rows : (block + 1) * own_rows]


def gather_sum(got, rows, blocks):
    width = got.shape[2]
    return pl.pallas_call(
        functools.partial(gather_sum_kernel, width // 2, rows, blocks),
        in_specs=[pl.BlockSpec(memory_space=pltpu.VMEM)],
        out_specs=[pl.BlockSpec(memory_space=pltpu.VMEM)] * len(blocks),
        out_shape=[pltpu.VMEM((len(group) * rows // 8, width), jnp.float32) for group in blocks],
        compiler_params=pltpu.CompilerParams(vmem_limit_bytes=16 * 2**20),
        name="gather_sum",
    )(got)


def swapped(value, mask):
    return lax.ppermute(value, "replica", [(source, source ^ mask) for source in range(lax.axis_size("replica"))])


def body(gradient, feedback, picked, counts, weights, moment, second):
    own_rows = weights.shape[0]
    reg_rows = own_rows * lax.axis_size("replica")
    tiles, new_feedback = pack(counts, picked, gradient, feedback)
    got = lax.all_to_all(tiles, "region", split_axis=0, concat_axis=0, tiled=True)
    far, four, seven, six, two, one, own = gather_sum(got, reg_rows, ((5, 3), (4,), (7,), (6,), (2,), (1,), (0,)))
    far = swapped(far, 3)
    six = six + far[:own_rows] + swapped(four, 2) + swapped(seven, 1)
    total = own + far[own_rows:] + swapped(six, 6) + swapped(two, 2) + swapped(one, 1)
    new_moment = 0.9 * moment + 0.1 * total
    new_second = 0.95 * second + 0.05 * total * total
    new_weights = weights - 0.02 * (new_moment / (jnp.sqrt(new_second) + 1e-08) + 0.1 * weights)
    return (new_weights, new_moment, new_second, new_feedback)


def solution(mesh):
    placed = (
        P("replica", "region", None, "tensor"),
        P("replica", "region", None, "tensor"),
        P("replica", "region", None, "tensor"),
        P("replica", "region", "tensor"),
        P(("region", "replica"), "tensor"),
        P(("region", "replica"), "tensor"),
        P(("region", "replica"), "tensor"),
    )
    return jax.shard_map(
        body,
        mesh=mesh,
        in_specs=placed,
        out_specs=(
            P(("region", "replica"), "tensor"),
            P(("region", "replica"), "tensor"),
            P(("region", "replica"), "tensor"),
            P("replica", "region", None, "tensor"),
        ),
        check_vma=False,
    )
```

```python
import functools

import jax
import jax.numpy as jnp
from jax import lax
from jax.experimental import pallas as pl
from jax.experimental.pallas import tpu as pltpu
from jax.sharding import PartitionSpec as P


def split(value):
    high = value.astype(jnp.bfloat16)
    low = (value - high.astype(jnp.float32)).astype(jnp.bfloat16)
    return jnp.concatenate([high, low], axis=1)


def one_hot(rows, ids):
    row = lax.broadcasted_iota(jnp.int32, (rows, ids.shape[1]), 0)
    return jnp.where(row == ids, 1.0, 0.0).astype(jnp.bfloat16)


def pack_kernel(chunks, counts_in, picked_in, gradient, feedback, tiles, new_feedback, near, counts, picked, hot, sems):
    owners, slots = picked.shape[2:]
    blocks, width = near.shape
    rows = blocks // owners
    step_rows = blocks // chunks
    pairs = owners // chunks // 2

    def copies(chunk):
        here = pl.ds(pl.multiple_of(chunk * step_rows, step_rows), step_rows)
        return (
            pltpu.make_async_copy(gradient.at[0, 0, here, :], near.at[here, :], sems.at[0, chunk]),
            pltpu.make_async_copy(feedback.at[0, 0, here, :], new_feedback.at[0, 0, here, :], sems.at[1, chunk]),
        )

    lists = (
        pltpu.make_async_copy(counts_in, counts, sems.at[2, 0]),
        pltpu.make_async_copy(picked_in, picked, sems.at[2, 1]),
    )
    for copy in lists:
        copy.start()
    for chunk in range(chunks):
        for copy in copies(chunk):
            copy.start()
    for copy in lists:
        copy.wait()
    lane = lax.broadcasted_iota(jnp.int32, (1, 2 * slots), 1)
    wide = (8, 2 * slots)
    lower = lax.broadcasted_iota(jnp.int32, wide, 1) < slots

    def prepare(pair, carry):
        first, second = 2 * pair, 2 * pair + 1
        ids = jnp.concatenate([picked[0, 0, pl.ds(first, 1), :], picked[0, 0, pl.ds(second, 1), :]], axis=1)
        limit = jnp.where(lane < slots, counts[0, 0, first], counts[0, 0, second] + slots)
        ids = jnp.where(lane < limit, ids, -1)
        hot[pair] = one_hot(rows, ids)
        sent = jnp.broadcast_to(ids.astype(jnp.float32), wide)
        turned = pltpu.roll(sent, slots, 1)
        tiles[pl.ds(first * (slots + 1) + slots, 1), :] = jnp.where(lower, sent, turned)[:1]
        tiles[pl.ds(second * (slots + 1) + slots, 1), :] = jnp.where(lower, turned, sent)[:1]
        return carry

    lax.fori_loop(0, owners // 2, prepare, 0, unroll=4)
    lower = lax.broadcasted_iota(jnp.int32, (2 * slots, width), 0) < slots
    ones = (jnp.where(lower, 1.0, 0.0).astype(jnp.bfloat16), jnp.where(lower, 0.0, 1.0).astype(jnp.bfloat16))

    def step(chunk, carry):
        for copy in copies(chunk):
            copy.wait()
        for part in range(2 * pairs):
            pair, side = chunk * pairs + part // 2, part % 2
            owner = 2 * pair + side
            here = pl.ds(pl.multiple_of(owner * rows, rows), rows)
            compensated = near[here, :].astype(jnp.float32) + new_feedback[0, 0, here, :]
            both = hot[pair]
            named = jnp.dot(both, ones[side], preferred_element_type=jnp.float32)
            new_feedback[0, 0, here, :] = jnp.where(named > 0.0, 0.0, compensated)
            halves = lax.dot_general(
                both, split(compensated), (((0,), (0,)), ((), ())), preferred_element_type=jnp.float32
            )[side * slots : (side + 1) * slots]
            tiles[pl.ds(owner * (slots + 1), slots), :] = halves[:, :width] + halves[:, width:]
        return carry

    lax.fori_loop(0, chunks, step, 0)


def pack(counts, picked, gradient, feedback):
    owners, slots = picked.shape[2:]
    blocks, width = gradient.shape[2:]
    chunks = 4
    arrays = [pltpu.with_memory_space_constraint(array, pltpu.HBM) for array in (counts, picked, gradient, feedback)]
    return pl.pallas_call(
        functools.partial(pack_kernel, chunks),
        in_specs=[pl.BlockSpec(memory_space=pltpu.HBM)] * 4,
        out_specs=[pl.BlockSpec(memory_space=pltpu.VMEM)] * 2,
        out_shape=[
            pltpu.VMEM((owners * (slots + 1), width), jnp.float32),
            pltpu.VMEM(feedback.shape, jnp.float32),
        ],
        scratch_shapes=[
            pltpu.VMEM((blocks, width), jnp.bfloat16),
            pltpu.SMEM(counts.shape, jnp.int32),
            pltpu.VMEM(picked.shape, jnp.int32),
            pltpu.VMEM((owners // 2, blocks // owners, 2 * slots), jnp.bfloat16),
            pltpu.SemaphoreType.DMA((3, chunks)),
        ],
        compiler_params=pltpu.CompilerParams(vmem_limit_bytes=32 * 2**20),
        name="pack",
    )(*arrays)


def gather_sum_kernel(slots, rows, blocks, got, *sums):
    me = lax.axis_index("replica")
    width = got.shape[1]
    sources = got.shape[0] // (slots + 1)
    own_rows = rows // 8
    lane = lax.broadcasted_iota(jnp.int32, (1, 2 * slots), 1)

    def numbers(source):
        return got[(source + 1) * (slots + 1) - 1 : (source + 1) * (slots + 1), :]

    def tile(source):
        return got[source * (slots + 1) : (source + 1) * (slots + 1) - 1, :]

    def hot(pair):
        first, second = 2 * pair, 2 * pair + 1
        ids = jnp.where(lane < slots, numbers(first), numbers(second)).astype(jnp.int32)
        return one_hot(rows, jnp.where(ids < 0, -1, ids ^ (me * own_rows)))

    halves = jnp.zeros((rows, 2 * width), jnp.float32)
    for pair in range(0, sources // 2, 2):
        named = jnp.concatenate([hot(pair), hot(pair + 1)], axis=1)
        parts = [split(tile(source)) for source in range(2 * pair, 2 * pair + 4)]
        halves += jnp.dot(named, jnp.concatenate(parts, axis=0), preferred_element_type=jnp.float32)
    total = halves[:, :width] + halves[:, width:]
    for group, ref in zip(blocks, sums):
        for position, block in enumerate(group):
            here = slice(position * own_rows, (position + 1) * own_rows)
            ref[here, :] = total[block * own_rows : (block + 1) * own_rows]


def gather_sum(got, slots, rows, blocks):
    width = got.shape[1]
    return pl.pallas_call(
        functools.partial(gather_sum_kernel, slots, rows, blocks),
        in_specs=[pl.BlockSpec(memory_space=pltpu.VMEM)],
        out_specs=[pl.BlockSpec(memory_space=pltpu.VMEM)] * len(blocks),
        out_shape=[pltpu.VMEM((len(group) * rows // 8, width), jnp.float32) for group in blocks],
        compiler_params=pltpu.CompilerParams(vmem_limit_bytes=16 * 2**20),
        name="gather_sum",
    )(pltpu.with_memory_space_constraint(got, pltpu.VMEM))


def swapped(value, mask):
    return lax.ppermute(value, "replica", [(source, source ^ mask) for source in range(lax.axis_size("replica"))])


def body(gradient, feedback, picked, counts, weights, moment, second):
    own_rows = weights.shape[0]
    reg_rows = own_rows * lax.axis_size("replica")
    tiles, new_feedback = pack(counts, picked, gradient, feedback)
    rows, width = tiles.shape
    got = lax.all_to_all(tiles.reshape(rows, 1, width), "region", split_axis=0, concat_axis=0, tiled=True)
    got = got.reshape(rows, width)
    far, four, seven, six, one, two, own = gather_sum(
        got, picked.shape[3], reg_rows, ((5, 3), (4,), (7,), (6,), (1,), (2,), (0,))
    )
    far = swapped(far, 3)
    six = six + far[:own_rows] + swapped(four, 2) + swapped(seven, 1)
    total = own + far[own_rows:] + swapped(six, 6) + swapped(one, 1) + swapped(two, 2)
    new_moment = 0.9 * moment + 0.1 * total
    new_second = 0.95 * second + 0.05 * total * total
    new_weights = weights - 0.02 * (new_moment / (jnp.sqrt(new_second) + 1e-08) + 0.1 * weights)
    return (new_weights, new_moment, new_second, new_feedback)


def solution(mesh):
    placed = (
        P("replica", "region", None, "tensor"),
        P("replica", "region", None, "tensor"),
        P("replica", "region", None, "tensor"),
        P("replica", "region", "tensor"),
        P(("region", "replica"), "tensor"),
        P(("region", "replica"), "tensor"),
        P(("region", "replica"), "tensor"),
    )
    return jax.shard_map(
        body,
        mesh=mesh,
        in_specs=placed,
        out_specs=(
            P(("region", "replica"), "tensor"),
            P(("region", "replica"), "tensor"),
            P(("region", "replica"), "tensor"),
            P("replica", "region", None, "tensor"),
        ),
        check_vma=False,
    )
```

```python
import functools

import jax
import jax.numpy as jnp
from jax import lax
from jax.experimental import pallas as pl
from jax.experimental.pallas import tpu as pltpu
from jax.sharding import PartitionSpec as P


def split(value):
    high = value.astype(jnp.bfloat16)
    low = (value - high.astype(jnp.float32)).astype(jnp.bfloat16)
    return jnp.concatenate([high, low], axis=1)


def one_hot(rows, ids):
    row = lax.broadcasted_iota(jnp.int32, (rows, ids.shape[1]), 0)
    return jnp.where(row == ids, 1.0, 0.0).astype(jnp.bfloat16)


def pack_kernel(chunks, counts_in, picked_in, gradient, feedback, tiles, new_feedback, near, counts, picked, hot, sems):
    owners, slots = picked.shape[2:]
    blocks, width = near.shape
    rows = blocks // owners
    step_rows = blocks // chunks
    pairs = owners // chunks // 2

    def copies(chunk):
        here = pl.ds(pl.multiple_of(chunk * step_rows, step_rows), step_rows)
        return (
            pltpu.make_async_copy(gradient.at[0, 0, here, :], near.at[here, :], sems.at[0, chunk]),
            pltpu.make_async_copy(feedback.at[0, 0, here, :], new_feedback.at[0, 0, here, :], sems.at[1, chunk]),
        )

    lists = (
        pltpu.make_async_copy(counts_in, counts, sems.at[2, 0]),
        pltpu.make_async_copy(picked_in, picked, sems.at[2, 1]),
    )
    for copy in lists:
        copy.start()
    for chunk in range(chunks):
        for copy in copies(chunk):
            copy.start()
    for copy in lists:
        copy.wait()
    lane = lax.broadcasted_iota(jnp.int32, (1, 2 * slots), 1)
    wide = (8, 2 * slots)
    lower = lax.broadcasted_iota(jnp.int32, wide, 1) < slots

    def prepare(pair, carry):
        first, second = 2 * pair, 2 * pair + 1
        ids = jnp.concatenate([picked[0, 0, pl.ds(first, 1), :], picked[0, 0, pl.ds(second, 1), :]], axis=1)
        limit = jnp.where(lane < slots, counts[0, 0, first], counts[0, 0, second] + slots)
        ids = jnp.where(lane < limit, ids, -1)
        hot[pair] = one_hot(rows, ids)
        sent = jnp.broadcast_to(ids.astype(jnp.float32), wide)
        turned = pltpu.roll(sent, slots, 1)
        tiles[pl.ds(first * (slots + 1) + slots, 1), :] = jnp.where(lower, sent, turned)[:1]
        tiles[pl.ds(second * (slots + 1) + slots, 1), :] = jnp.where(lower, turned, sent)[:1]
        return carry

    lax.fori_loop(0, owners // 2, prepare, 0, unroll=4)
    column = lax.broadcasted_iota(jnp.int32, (2 * slots, 2 * width), 1) < width
    lower = lax.broadcasted_iota(jnp.int32, (2 * slots, 2 * width), 0) < slots
    ones = jnp.where(lower == column, 1.0, 0.0).astype(jnp.bfloat16)

    def step(chunk, carry):
        for copy in copies(chunk):
            copy.wait()
        for part in range(pairs):
            pair = chunk * pairs + part
            both = hot[pair]
            named = jnp.dot(both, ones, preferred_element_type=jnp.float32)
            for side in (0, 1):
                owner = 2 * pair + side
                here = pl.ds(pl.multiple_of(owner * rows, rows), rows)
                compensated = near[here, :].astype(jnp.float32) + new_feedback[0, 0, here, :]
                own = named[:, side * width : (side + 1) * width]
                new_feedback[0, 0, here, :] = jnp.where(own > 0.0, 0.0, compensated)
                halves = lax.dot_general(
                    both, split(compensated), (((0,), (0,)), ((), ())), preferred_element_type=jnp.float32
                )[side * slots : (side + 1) * slots]
                tiles[pl.ds(owner * (slots + 1), slots), :] = halves[:, :width] + halves[:, width:]
        return carry

    lax.fori_loop(0, chunks, step, 0)


def pack(counts, picked, gradient, feedback):
    owners, slots = picked.shape[2:]
    blocks, width = gradient.shape[2:]
    chunks = 4
    arrays = [pltpu.with_memory_space_constraint(array, pltpu.HBM) for array in (counts, picked, gradient, feedback)]
    return pl.pallas_call(
        functools.partial(pack_kernel, chunks),
        in_specs=[pl.BlockSpec(memory_space=pltpu.HBM)] * 4,
        out_specs=[pl.BlockSpec(memory_space=pltpu.VMEM)] * 2,
        out_shape=[
            pltpu.VMEM((owners * (slots + 1), width), jnp.float32),
            pltpu.VMEM(feedback.shape, jnp.float32),
        ],
        scratch_shapes=[
            pltpu.VMEM((blocks, width), jnp.bfloat16),
            pltpu.SMEM(counts.shape, jnp.int32),
            pltpu.VMEM(picked.shape, jnp.int32),
            pltpu.VMEM((owners // 2, blocks // owners, 2 * slots), jnp.bfloat16),
            pltpu.SemaphoreType.DMA((3, chunks)),
        ],
        compiler_params=pltpu.CompilerParams(vmem_limit_bytes=32 * 2**20),
        name="pack",
    )(*arrays)


def gather_sum_kernel(slots, rows, blocks, got, *sums):
    me = lax.axis_index("replica")
    width = got.shape[1]
    sources = got.shape[0] // (slots + 1)
    own_rows = rows // 8
    lane = lax.broadcasted_iota(jnp.int32, (1, 2 * slots), 1)

    def numbers(source):
        return got[(source + 1) * (slots + 1) - 1 : (source + 1) * (slots + 1), :]

    def tile(source):
        return got[source * (slots + 1) : (source + 1) * (slots + 1) - 1, :]

    def hot(pair):
        first, second = 2 * pair, 2 * pair + 1
        ids = jnp.where(lane < slots, numbers(first), numbers(second)).astype(jnp.int32)
        return one_hot(rows, jnp.where(ids < 0, -1, ids ^ (me * own_rows)))

    halves = jnp.zeros((rows, 2 * width), jnp.float32)
    for pair in range(0, sources // 2, 2):
        named = jnp.concatenate([hot(pair), hot(pair + 1)], axis=1)
        parts = [split(tile(source)) for source in range(2 * pair, 2 * pair + 4)]
        halves += jnp.dot(named, jnp.concatenate(parts, axis=0), preferred_element_type=jnp.float32)
    total = halves[:, :width] + halves[:, width:]
    for group, ref in zip(blocks, sums):
        for position, block in enumerate(group):
            here = slice(position * own_rows, (position + 1) * own_rows)
            ref[here, :] = total[block * own_rows : (block + 1) * own_rows]


def gather_sum(got, slots, rows, blocks):
    width = got.shape[1]
    return pl.pallas_call(
        functools.partial(gather_sum_kernel, slots, rows, blocks),
        in_specs=[pl.BlockSpec(memory_space=pltpu.VMEM)],
        out_specs=[pl.BlockSpec(memory_space=pltpu.VMEM)] * len(blocks),
        out_shape=[pltpu.VMEM((len(group) * rows // 8, width), jnp.float32) for group in blocks],
        compiler_params=pltpu.CompilerParams(vmem_limit_bytes=16 * 2**20),
        name="gather_sum",
    )(pltpu.with_memory_space_constraint(got, pltpu.VMEM))


def swapped(value, mask):
    return lax.ppermute(value, "replica", [(source, source ^ mask) for source in range(lax.axis_size("replica"))])


def body(gradient, feedback, picked, counts, weights, moment, second):
    own_rows = weights.shape[0]
    reg_rows = own_rows * lax.axis_size("replica")
    tiles, new_feedback = pack(counts, picked, gradient, feedback)
    rows, width = tiles.shape
    got = lax.all_to_all(tiles.reshape(rows, 1, width), "region", split_axis=0, concat_axis=0, tiled=True)
    got = got.reshape(rows, width)
    far, four, seven, six, one, two, own = gather_sum(
        got, picked.shape[3], reg_rows, ((5, 3), (4,), (7,), (6,), (1,), (2,), (0,))
    )
    far = swapped(far, 3)
    six = six + far[:own_rows] + swapped(four, 2) + swapped(seven, 1)
    total = own + far[own_rows:] + swapped(six, 6) + swapped(one, 1) + swapped(two, 2)
    new_moment = 0.9 * moment + 0.1 * total
    new_second = 0.95 * second + 0.05 * total * total
    new_weights = weights - 0.02 * (new_moment / (jnp.sqrt(new_second) + 1e-08) + 0.1 * weights)
    return (new_weights, new_moment, new_second, new_feedback)


def solution(mesh):
    placed = (
        P("replica", "region", None, "tensor"),
        P("replica", "region", None, "tensor"),
        P("replica", "region", None, "tensor"),
        P("replica", "region", "tensor"),
        P(("region", "replica"), "tensor"),
        P(("region", "replica"), "tensor"),
        P(("region", "replica"), "tensor"),
    )
    return jax.shard_map(
        body,
        mesh=mesh,
        in_specs=placed,
        out_specs=(
            P(("region", "replica"), "tensor"),
            P(("region", "replica"), "tensor"),
            P(("region", "replica"), "tensor"),
            P("replica", "region", None, "tensor"),
        ),
        check_vma=False,
    )
```

```python
import functools

import jax
import jax.numpy as jnp
from jax import lax
from jax.experimental import pallas as pl
from jax.experimental.pallas import tpu as pltpu
from jax.sharding import PartitionSpec as P


def split(value):
    high = value.astype(jnp.bfloat16)
    low = (value - high.astype(jnp.float32)).astype(jnp.bfloat16)
    return jnp.concatenate([high, low], axis=1)


def one_hot(rows, ids):
    row = lax.broadcasted_iota(jnp.int32, (rows, ids.shape[1]), 0)
    return jnp.where(row == ids, 1.0, 0.0).astype(jnp.bfloat16)


def pack_kernel(chunks, counts_in, picked_in, gradient, feedback, tiles, new_feedback, near, counts, picked, hot, sems):
    owners, slots = picked.shape[2:]
    blocks, width = near.shape
    rows = blocks // owners
    step_rows = blocks // chunks
    pairs = owners // chunks // 2

    def copies(chunk):
        here = pl.ds(pl.multiple_of(chunk * step_rows, step_rows), step_rows)
        return (
            pltpu.make_async_copy(gradient.at[0, 0, here, :], near.at[here, :], sems.at[0, chunk]),
            pltpu.make_async_copy(feedback.at[0, 0, here, :], new_feedback.at[0, 0, here, :], sems.at[1, chunk]),
        )

    lists = (
        pltpu.make_async_copy(counts_in, counts, sems.at[2, 0]),
        pltpu.make_async_copy(picked_in, picked, sems.at[2, 1]),
    )
    for copy in lists:
        copy.start()
    for chunk in range(chunks):
        for copy in copies(chunk):
            copy.start()
    for copy in lists:
        copy.wait()
    lane = lax.broadcasted_iota(jnp.int32, (1, 2 * slots), 1)
    wide = (8, 2 * slots)
    lower = lax.broadcasted_iota(jnp.int32, wide, 1) < slots

    def prepare(pair, carry):
        first, second = 2 * pair, 2 * pair + 1
        ids = jnp.concatenate([picked[0, 0, pl.ds(first, 1), :], picked[0, 0, pl.ds(second, 1), :]], axis=1)
        limit = jnp.where(lane < slots, counts[0, 0, first], counts[0, 0, second] + slots)
        ids = jnp.where(lane < limit, ids, -1)
        hot[pair] = one_hot(rows, ids)
        sent = jnp.broadcast_to(ids.astype(jnp.float32), wide)
        turned = pltpu.roll(sent, slots, 1)
        tiles[pl.ds(first * (slots + 1) + slots, 1), :] = jnp.where(lower, sent, turned)[:1]
        tiles[pl.ds(second * (slots + 1) + slots, 1), :] = jnp.where(lower, turned, sent)[:1]
        return carry

    lax.fori_loop(0, owners // 2, prepare, 0, unroll=4)
    lower = lax.broadcasted_iota(jnp.int32, (2 * slots, width), 0) < slots
    ones = (jnp.where(lower, 1.0, 0.0).astype(jnp.bfloat16), jnp.where(lower, 0.0, 1.0).astype(jnp.bfloat16))

    def step(chunk, carry):
        for copy in copies(chunk):
            copy.wait()
        for part in range(2 * pairs):
            pair, side = chunk * pairs + part // 2, part % 2
            owner = 2 * pair + side
            here = pl.ds(pl.multiple_of(owner * rows, rows), rows)
            compensated = near[here, :].astype(jnp.float32) + new_feedback[0, 0, here, :]
            both = hot[pair]
            named = jnp.dot(both, ones[side], preferred_element_type=jnp.float32)
            new_feedback[0, 0, here, :] = jnp.where(named > 0.0, 0.0, compensated)
            halves = lax.dot_general(
                both, split(compensated), (((0,), (0,)), ((), ())), preferred_element_type=jnp.float32
            )[side * slots : (side + 1) * slots]
            tiles[pl.ds(owner * (slots + 1), slots), :] = halves[:, :width] + halves[:, width:]
        return carry

    lax.fori_loop(0, chunks, step, 0)


def pack(counts, picked, gradient, feedback):
    owners, slots = picked.shape[2:]
    blocks, width = gradient.shape[2:]
    chunks = 4
    arrays = [pltpu.with_memory_space_constraint(array, pltpu.HBM) for array in (counts, picked, gradient, feedback)]
    return pl.pallas_call(
        functools.partial(pack_kernel, chunks),
        in_specs=[pl.BlockSpec(memory_space=pltpu.HBM)] * 4,
        out_specs=[pl.BlockSpec(memory_space=pltpu.VMEM)] * 2,
        out_shape=[
            pltpu.VMEM((owners * (slots + 1), width), jnp.float32),
            pltpu.VMEM(feedback.shape, jnp.float32),
        ],
        scratch_shapes=[
            pltpu.VMEM((blocks, width), jnp.bfloat16),
            pltpu.SMEM(counts.shape, jnp.int32),
            pltpu.VMEM(picked.shape, jnp.int32),
            pltpu.VMEM((owners // 2, blocks // owners, 2 * slots), jnp.bfloat16),
            pltpu.SemaphoreType.DMA((3, chunks)),
        ],
        compiler_params=pltpu.CompilerParams(vmem_limit_bytes=32 * 2**20),
        name="pack",
    )(*arrays)


def gather_sum_kernel(slots, rows, blocks, got, *sums):
    me = lax.axis_index("replica")
    width = got.shape[1]
    sources = got.shape[0] // (slots + 1)
    own_rows = rows // 8
    lane = lax.broadcasted_iota(jnp.int32, (1, 2 * slots), 1)

    def numbers(source):
        return got[(source + 1) * (slots + 1) - 1 : (source + 1) * (slots + 1), :]

    def tile(source):
        return got[source * (slots + 1) : (source + 1) * (slots + 1) - 1, :]

    def hot(pair):
        first, second = 2 * pair, 2 * pair + 1
        ids = jnp.where(lane < slots, numbers(first), numbers(second)).astype(jnp.int32)
        return one_hot(rows, jnp.where(ids < 0, -1, ids ^ (me * own_rows)))

    halves = jnp.zeros((rows, 2 * width), jnp.float32)
    for pair in range(0, sources // 2, 4):
        named = jnp.concatenate([hot(pair + more) for more in range(4)], axis=1)
        parts = [split(tile(source)) for source in range(2 * pair, 2 * pair + 8)]
        halves += jnp.dot(named, jnp.concatenate(parts, axis=0), preferred_element_type=jnp.float32)
    total = halves[:, :width] + halves[:, width:]
    for group, ref in zip(blocks, sums):
        for position, block in enumerate(group):
            here = slice(position * own_rows, (position + 1) * own_rows)
            ref[here, :] = total[block * own_rows : (block + 1) * own_rows]


def gather_sum(got, slots, rows, blocks):
    width = got.shape[1]
    return pl.pallas_call(
        functools.partial(gather_sum_kernel, slots, rows, blocks),
        in_specs=[pl.BlockSpec(memory_space=pltpu.VMEM)],
        out_specs=[pl.BlockSpec(memory_space=pltpu.VMEM)] * len(blocks),
        out_shape=[pltpu.VMEM((len(group) * rows // 8, width), jnp.float32) for group in blocks],
        compiler_params=pltpu.CompilerParams(vmem_limit_bytes=16 * 2**20),
        name="gather_sum",
    )(pltpu.with_memory_space_constraint(got, pltpu.VMEM))


def swapped(value, mask):
    return lax.ppermute(value, "replica", [(source, source ^ mask) for source in range(lax.axis_size("replica"))])


def body(gradient, feedback, picked, counts, weights, moment, second):
    own_rows = weights.shape[0]
    reg_rows = own_rows * lax.axis_size("replica")
    tiles, new_feedback = pack(counts, picked, gradient, feedback)
    rows, width = tiles.shape
    got = lax.all_to_all(tiles.reshape(rows, 1, width), "region", split_axis=0, concat_axis=0, tiled=True)
    got = got.reshape(rows, width)
    far, four, seven, six, one, two, own = gather_sum(
        got, picked.shape[3], reg_rows, ((5, 3), (4,), (7,), (6,), (1,), (2,), (0,))
    )
    far = swapped(far, 3)
    six = six + far[:own_rows] + swapped(four, 2) + swapped(seven, 1)
    total = own + far[own_rows:] + swapped(six, 6) + swapped(one, 1) + swapped(two, 2)
    new_moment = 0.9 * moment + 0.1 * total
    new_second = 0.95 * second + 0.05 * total * total
    new_weights = weights - 0.02 * (new_moment / (jnp.sqrt(new_second) + 1e-08) + 0.1 * weights)
    return (new_weights, new_moment, new_second, new_feedback)


def solution(mesh):
    placed = (
        P("replica", "region", None, "tensor"),
        P("replica", "region", None, "tensor"),
        P("replica", "region", None, "tensor"),
        P("replica", "region", "tensor"),
        P(("region", "replica"), "tensor"),
        P(("region", "replica"), "tensor"),
        P(("region", "replica"), "tensor"),
    )
    return jax.shard_map(
        body,
        mesh=mesh,
        in_specs=placed,
        out_specs=(
            P(("region", "replica"), "tensor"),
            P(("region", "replica"), "tensor"),
            P(("region", "replica"), "tensor"),
            P("replica", "region", None, "tensor"),
        ),
        check_vma=False,
    )
```
